512 devices in a mesh: dp: 64 (over z, x), tensor: 8 (over y, core).
Axes of the slice: x: 4, y: 4, z: 16, core: 2. Of those that a mesh axis runs over, the one named last changes fastest.
Arguments:
- queries: bfloat16 [4096, 8, 32, 128], P('dp', None, 'tensor'), may hold values from -8 to 8
- keys_new: bfloat16 [4096, 8, 8, 128], P('dp', None, 'tensor'), may hold values from -6 to 6
- values_new: bfloat16 [4096, 8, 8, 128], P('dp', None, 'tensor'), may hold values from -6 to 6
- residual: bfloat16 [4096, 8, 4096], P('dp', None, 'tensor'), may hold values from -4 to 4
- cand_len: int32 [4096], P('dp'), may hold values from 1 to 8, as said below
- owner_map: int32 [4096], P('dp'), may hold values from 0 to 63, as said below
- prompt_len: int32 [64], P('dp'), may hold values from 2 to 2048, as said below
- keys_cache: bfloat16 [64, 2048, 8, 128], P('dp', None, 'tensor'), may hold values from -6 to 6
- values_cache: bfloat16 [64, 2048, 8, 128], P('dp', None, 'tensor'), may hold values from -6 to 6
- norm_gain: bfloat16 [4096], P('tensor'), may hold values from 0.099609375 to 1.8984375
- value_head: bfloat16 [4096], P('tensor'), may hold values from -0.09375 to 0.09375
Outputs:
- values: float32 [4096, 8], P('dp')
The draws below stay inside these ranges and needn't reach their ends.
Inputs may be any that keep to these rules, and one draw needn't show every extreme that they name: `owner_map`: at most 2 of the 64 candidates held by one dp index share a prompt; each prompt has at most 128 candidates in all, and some prompt has exactly 128, 2 from every dp index. `cand_len`: token slots at or past a candidate's length are padding; some candidate has all 8. `prompt_len`: cache rows at or past a prompt's length are unused; some prompt has all 2048.
All inputs are finite; a program needn't handle non-finite values.
Results may differ from the reference program's by a relative error of at most 0.0032.
Values may be sent and summed in bfloat16 or wider, within the bound.
A program may use at most 64 MiB of HBM per device.

```python
import math
import jax
import jax.numpy as jnp
from jax import lax

QH = 32
KVH = 8
HD = 128
L = 8
PMAX = 2048
FEAT = 4096
CANDS = 4096
PROMPTS = 64
N_DP = 64


def draw_queries(key, part):
    key = jax.random.fold_in(key, 11)
    key_one = jax.random.fold_in(key, 0)
    extent = (CANDS, L, QH, HD)
    drawn_values = jnp.clip(jax.random.normal(key_one, extent, jnp.float32), -6.0, 6.0)
    return drawn_values.astype(jnp.bfloat16)


def draw_keys_cache(key, part):
    key = jax.random.fold_in(key, 12)
    extent = (PROMPTS, PMAX, KVH, HD)
    drawn_values = jnp.clip(jax.random.normal(key, extent, jnp.float32), -6.0, 6.0)
    return drawn_values.astype(jnp.bfloat16)


def draw_residual(key, part):
    key = jax.random.fold_in(key, 13)
    key_one, key_two, key_three = jax.random.split(key, 3)
    extent = (CANDS, L, FEAT)
    position = jnp.arange(FEAT).astype(jnp.float32) / FEAT
    trend = 0.5
    noise_part = jnp.clip(jax.random.normal(key_one, extent, jnp.float32), -4.0, 4.0)
    column = 10.0 ** (0.8 * jax.random.uniform(key_two, (FEAT,), jnp.float32)) * 3.0 ** (trend * position)
    row_scale = 10.0 ** jax.random.uniform(key_three, (CANDS, L, 1), jnp.float32)
    return (0.003 * noise_part * column * row_scale).astype(jnp.bfloat16)


def draw_owner_map(key, part):
    key = jax.random.fold_in(key, 14)
    key_one, key_two, key_three, key_four, key_five = jax.random.split(key, 5)
    per_source = N_DP
    pair_count = N_DP // 2
    offsets = jax.random.randint(key_one, (pair_count,), 0, per_source + 1)
    hottest = jax.random.randint(key_two, (), 0, pair_count)
    offsets = jnp.where(jnp.arange(pair_count) == hottest, per_source, offsets)
    load_per = jnp.stack([per_source - offsets, per_source + offsets], axis=1).reshape(N_DP)
    bounds = jnp.cumsum(load_per)
    entries = jnp.arange(N_DP * per_source)
    owners = jnp.sum((entries[:, None] >= bounds[None, :]).astype(jnp.int32), axis=1)
    owner_table = owners.reshape(per_source, N_DP).T
    relabel = jax.random.permutation(key_three, N_DP)
    owner_table = relabel[owner_table]
    owner_table = owner_table[jax.random.permutation(key_four, N_DP)]
    tie_noise = jax.random.randint(key_five, (N_DP, per_source), 0, 2 ** 20) * per_source + jnp.arange(per_source)[None, :]
    new_order = jnp.argsort(tie_noise, axis=1, stable=True)
    owner_table = jnp.take_along_axis(owner_table, new_order, axis=1)
    return owner_table.reshape(N_DP * per_source).astype(jnp.int32)


def draw_cand_len(key, part):
    key = jax.random.fold_in(key, 15)
    key_one, key_two = jax.random.split(key)
    lengths = jax.random.randint(key_one, (CANDS,), 1, L + 1)
    forced = jax.random.randint(key_two, (), 0, CANDS)
    return jnp.where(jnp.arange(CANDS) == forced, L, lengths).astype(jnp.int32)


def draw_prompt_len(key, part):
    key = jax.random.fold_in(key, 16)
    key_one, key_two = jax.random.split(key)
    lengths = jax.random.randint(key_one, (PROMPTS,), 2, PMAX + 1)
    forced = jax.random.randint(key_two, (), 0, PROMPTS)
    return jnp.where(jnp.arange(PROMPTS) == forced, PMAX, lengths).astype(jnp.int32)


def block_levels(own_key, shape, pieces, low, largest):
    loudness = 1.0
    for dim, shards_of in pieces:
        heights = jax.random.uniform(jax.random.fold_in(jax.random.fold_in(own_key, 6), dim), (shards_of,), jnp.float32, low / len(pieces), largest / len(pieces))
        loudness = loudness * jnp.repeat(jnp.exp(heights), shape[dim] // shards_of).reshape((-1,) + (1,) * (len(shape) - 1 - dim))
    return loudness


def noise(rng, dims, spread, reach, pieces=(), held_as=jnp.bfloat16):
    drawn = spread * jax.random.normal(rng, dims, jnp.float32)
    if pieces:
        drawn = drawn * block_levels(rng, dims, pieces, -0.22, 0.18)
    return jnp.clip(drawn, -reach, reach).astype(held_as)


def setup_inputs(seed: int = 0) -> dict:
    arg_keys = jax.random.split(jax.random.key(seed), 12)
    queries = draw_queries(jax.random.fold_in(arg_keys[11], 71), 0)
    keys_new = noise(arg_keys[1], (CANDS, L, KVH, HD), 1.0, 6.0, ((0, 64), (2, 8)))
    values_new = noise(arg_keys[2], (CANDS, L, KVH, HD), 1.0, 6.0, ((0, 64), (2, 8)))
    residual = draw_residual(jax.random.fold_in(arg_keys[11], 71), 0)
    cand_len = draw_cand_len(jax.random.fold_in(arg_keys[11], 71), 0)
    owner_map = draw_owner_map(jax.random.fold_in(arg_keys[11], 71), 0)
    prompt_len = draw_prompt_len(jax.random.fold_in(arg_keys[11], 71), 0)
    keys_cache = draw_keys_cache(jax.random.fold_in(arg_keys[11], 71), 0)
    values_cache = noise(arg_keys[8], (PROMPTS, PMAX, KVH, HD), 1.0, 6.0, ((0, 64), (2, 8)))
    norm_gain = jnp.clip(1.0 + 0.18 * jax.random.normal(arg_keys[9], (FEAT,), jnp.float32), 0.099609375, 1.8984375).astype(jnp.bfloat16)
    value_head = noise(arg_keys[10], (FEAT,), FEAT ** -0.5, 0.09375, ((0, 8),))
    return dict(queries=queries, keys_new=keys_new, values_new=values_new, residual=residual, cand_len=cand_len, owner_map=owner_map, prompt_len=prompt_len, keys_cache=keys_cache, values_cache=values_cache, norm_gain=norm_gain, value_head=value_head)


EPSILON = 1e-05

def score_candidate(cand_index, queries, keys_new, values_new, residual, cand_len, owner_map, prompt_len, keys_cache, values_cache, norm_gain, value_head):
    group_size = QH // KVH
    scaling = 1.0 / math.sqrt(HD)
    prompt = owner_map[cand_index].astype(jnp.int32)
    query_rows = queries[cand_index].astype(jnp.float32).reshape(L, KVH, group_size, HD)
    new_keys = keys_new[cand_index].astype(jnp.float32)
    new_values = values_new[cand_index].astype(jnp.float32)
    cache_keys = lax.dynamic_index_in_dim(keys_cache, prompt, 0, keepdims=False).astype(jnp.float32)
    cache_values = lax.dynamic_index_in_dim(values_cache, prompt, 0, keepdims=False).astype(jnp.float32)
    prompt_size = lax.dynamic_index_in_dim(prompt_len, prompt, 0, keepdims=False)
    cand_size = cand_len[cand_index]
    prefix_scores = jnp.einsum('lkgd,pkd->kglp', query_rows, cache_keys) * scaling
    prefix_mask = jnp.arange(PMAX, dtype=jnp.int32) < prompt_size
    prefix_scores = jnp.where(prefix_mask, prefix_scores, -jnp.inf)
    own_scores = jnp.einsum('lkgd,mkd->kglm', query_rows, new_keys) * scaling
    causal = jnp.arange(L, dtype=jnp.int32)[:, None] >= jnp.arange(L, dtype=jnp.int32)[None, :]
    own_scores = jnp.where(causal, own_scores, -jnp.inf)
    highest = jnp.maximum(lax.optimization_barrier(jnp.max(prefix_scores, axis=-1)), lax.optimization_barrier(jnp.max(own_scores, axis=-1)))
    exp_prefix = jnp.exp(prefix_scores - highest[..., None])
    exp_own = jnp.exp(own_scores - highest[..., None])
    denominator = lax.optimization_barrier(jnp.sum(exp_prefix, axis=-1)) + lax.optimization_barrier(jnp.sum(exp_own, axis=-1))
    weight_prefix = (exp_prefix / denominator[..., None]).astype(jnp.bfloat16)
    weight_own = (exp_own / denominator[..., None]).astype(jnp.bfloat16)
    weight_prefix = lax.optimization_barrier(weight_prefix).astype(jnp.float32)
    weight_own = lax.optimization_barrier(weight_own).astype(jnp.float32)
    mixed = jnp.einsum('kglp,pkd->lkgd', weight_prefix, cache_values) + jnp.einsum('kglm,mkd->lkgd', weight_own, new_values)
    mixed = mixed.reshape(L, QH * HD).astype(jnp.bfloat16)
    hidden = residual[cand_index].astype(jnp.float32) + mixed.astype(jnp.float32)
    mean_square = lax.optimization_barrier(jnp.mean(hidden * hidden, axis=-1))
    normed = hidden * lax.rsqrt(mean_square + EPSILON)[:, None]
    scored = lax.optimization_barrier(jnp.sum(normed * norm_gain.astype(jnp.float32) * value_head.astype(jnp.float32), axis=-1))
    return jnp.where(jnp.arange(L, dtype=jnp.int32) < cand_size, scored, jnp.zeros_like(scored))

def reference(queries, keys_new, values_new, residual, cand_len, owner_map, prompt_len, keys_cache, values_cache, norm_gain, value_head):

    def per_candidate(cand_index):
        return score_candidate(cand_index, queries, keys_new, values_new, residual, cand_len, owner_map, prompt_len, keys_cache, values_cache, norm_gain, value_head)
    return lax.map(per_candidate, jnp.arange(CANDS, dtype=jnp.int32))
```

```python
import functools
import math

import jax
import jax.numpy as jnp
from jax import lax
from jax.experimental import pallas as pl
from jax.experimental.pallas import tpu as pltpu
from jax.sharding import PartitionSpec as P

EPSILON = 1e-05
MESH = pl.DeviceIdType.MESH
NZ = 16
NX = 4
NT = 8
RANKS = 2
GROUPS = NZ
PAIR = NX * RANKS
SLOTS = GROUPS * PAIR
LENGTH = 8
HEADS = 4
ROWS = HEADS * LENGTH
HD = 128
PMAX = 2048
CANDS = 64
FEATURES = 4096
MASKED = -1e30
LOG2E = math.log2(math.e)


def iota(shape, dim):
    return lax.broadcasted_iota(jnp.int32, shape, dim)


def group_dz(group):
    size = 8 - (group + 1) // 2
    return lax.rem(NZ + (2 * lax.rem(group, 2) - 1) * size, NZ)


def kernel(
    owner_ref,
    len_ref,
    weight_ref,
    plen_ref,
    q_hbm,
    kn_hbm,
    vn_hbm,
    res_hbm,
    kc_hbm,
    vc_hbm,
    out_ref,
    q_in,
    kn,
    vn,
    res,
    kc,
    vc,
    q_perm,
    q_out,
    q_got,
    m_out,
    m_got,
    l_out,
    l_got,
    own_o,
    own_l,
    bias,
    idx_v,
    idx_s,
    place,
    acc,
    part,
    load_sem,
    idx_sem,
    q_ssem,
    q_rsem,
    m_ssem,
    m_rsem,
    l_ssem,
    l_rsem,
    p_ssem,
    p_rsem,
):
    me = lax.axis_index("dp")
    my_t = lax.axis_index("tensor")
    my_z, my_x = lax.div(me, NX), lax.rem(me, NX)

    def partner(dz, dx):
        return lax.rem(my_z + dz, NZ) * NX + lax.rem(my_x + dx, NX)

    barrier = pltpu.get_barrier_semaphore()

    def greet(offset, carry):
        other = lax.rem(me + offset, NZ * NX)
        pl.semaphore_signal(barrier, inc=1, device_id={"dp": other}, device_id_type=MESH)
        return carry

    lax.fori_loop(1, NZ * NX, greet, 0)
    for offset in range(1, NT):
        pl.semaphore_signal(
            barrier,
            inc=1,
            device_id={"tensor": lax.rem(my_t + offset, NT)},
            device_id_type=MESH,
        )

    loads = [
        pltpu.make_async_copy(source, target, load_sem.at[n])
        for n, (source, target) in enumerate(
            [(q_hbm, q_in), (kn_hbm, kn), (vn_hbm, vn), (kc_hbm, kc), (vc_hbm, vc), (res_hbm, res)]
        )
    ]
    for load in loads:
        load.start()

    lane = iota((128, 128), 1)
    row = iota((128, 128), 0)
    owner = jnp.broadcast_to(owner_ref[...], (128, 128))
    dz = lax.rem(lax.div(owner, NX) - my_z + NZ, NZ)
    dx = lax.rem(lax.rem(owner, NX) - my_x + NX, NX)
    group = jnp.where(dz < NZ // 2, NZ - 1 - 2 * dz, 2 * dz - NZ)
    pair_lane = jnp.where(lane < CANDS, group * NX + dx, 1000 + lane)
    pair_row = pair_lane.T
    same = pair_lane == pair_row
    rank_lane = jnp.sum(jnp.where(same & (row < lane), 1, 0), axis=0, keepdims=True)
    rank_row = jnp.sum(jnp.where(same & (lane < row), 1, 0), axis=1, keepdims=True)
    slot_lane = pair_lane * RANKS + rank_lane
    slot_row = pair_row * RANKS + rank_row
    place[...] = jnp.where(row == slot_lane, 1.0, 0.0).astype(jnp.bfloat16)
    chosen = jnp.sum(jnp.where(slot_row == lane, row, 0), axis=0, keepdims=True)
    idx_v[...] = jnp.broadcast_to(chosen, (8, 128))
    fetch = pltpu.make_async_copy(idx_v, idx_s, idx_sem)
    fetch.start()

    to_row = iota((256, 256), 0)
    from_row = iota((256, 256), 1)
    source_row = (to_row // ROWS) * ROWS + (to_row % LENGTH) * HEADS + (to_row % ROWS) // LENGTH
    shuffle = jnp.where(from_row == source_row, 1.0, 0.0).astype(jnp.bfloat16)
    loads[0].wait()

    def reorder(n, carry):
        rows = q_in[pl.ds(n * 8, 8)].reshape(256, HD)
        mixed = jnp.dot(shuffle, rows, preferred_element_type=jnp.float32)
        q_perm[pl.ds(n * 8, 8)] = mixed.astype(jnp.bfloat16).reshape(8, ROWS, HD)
        return carry

    lax.fori_loop(0, CANDS // 8, reorder, 0)
    fetch.wait()

    def pack(group, carry):
        for n in range(PAIR):
            slot = group * PAIR + n
            q_out[slot] = q_perm[idx_s[0, slot]]
        return carry

    lax.fori_loop(0, GROUPS, pack, 0)

    pl.semaphore_wait(barrier, NZ * NX - 1 + NT - 1)

    def span(ref, group, dx, per):
        return ref.at[pl.ds((group * NX + dx) * per, per)]

    def remote(source, target, ssem, rsem, group, dx, per, forth):
        dz = group_dz(group)
        to = partner(dz, dx) if forth else partner(NZ - dz, NX - dx)
        return pltpu.make_async_remote_copy(
            src_ref=span(source, group, dx, per),
            dst_ref=span(target, group, dx, per),
            send_sem=ssem.at[group],
            recv_sem=rsem.at[group],
            device_id={"dp": to},
            device_id_type=MESH,
        )

    last = GROUPS - 1

    def keep(source, target, rsem, per):
        return pltpu.make_async_copy(
            span(source, last, 0, per), span(target, last, 0, per), rsem.at[last]
        )

    def send(source, target, ssem, rsem, group, per, forth):
        for dx in range(1, NX):
            remote(source, target, ssem, rsem, group, dx, per, forth).start()

        @pl.when(group != last)
        def _():
            remote(source, target, ssem, rsem, group, 0, per, forth).start()

        @pl.when(group == last)
        def _():
            keep(source, target, rsem, per).start()

    def arrived(target, rsem, group, per):
        whole = target.at[pl.ds(group * NX * per, NX * per)]
        pltpu.make_async_copy(whole, whole, rsem.at[group]).wait()

    def send_query(n, carry):
        group = lax.rem(n + last, GROUPS)
        send(q_out, q_got, q_ssem, q_rsem, group, RANKS, True)
        return carry

    lax.fori_loop(0, GROUPS, send_query, 0)

    scale = LOG2E / math.sqrt(HD)

    def softmax_values(scores, value_rows):
        highest = jnp.max(scores, axis=1, keepdims=True)
        powers = jnp.exp2(scores - highest)
        total = jnp.sum(powers, axis=1, keepdims=True)
        sums = jnp.dot(powers.astype(jnp.bfloat16), value_rows, preferred_element_type=jnp.float32)
        return sums / total, highest + jnp.log2(total)

    def scores_of(query_rows, key_rows):
        return (
            lax.dot_general(
                query_rows, key_rows, (((1,), (1,)), ((), ())), preferred_element_type=jnp.float32
            )
            * scale
        )

    loads[1].wait()
    loads[2].wait()
    at_row = iota((512, 128), 0)
    at_key = iota((512, 128), 1)
    seen = (at_row // ROWS == at_key // LENGTH) & (at_key % LENGTH <= at_row % LENGTH)

    def own_tokens(n, carry):
        rows = q_perm[pl.ds(n * 16, 16)].reshape(512, HD)
        scores = scores_of(rows, kn[pl.ds(n * 128, 128)])
        scores = jnp.where(seen, scores, MASKED)
        averages, logs = softmax_values(scores, vn[pl.ds(n * 128, 128)])
        own_o[pl.ds(n * 16, 16)] = averages.reshape(16, ROWS, HD)
        own_l[pl.ds(n * 16, 16)] = jnp.broadcast_to(logs, (512, HD)).reshape(16, ROWS, HD)
        return carry

    lax.fori_loop(0, CANDS // 16, own_tokens, 0)

    loads[3].wait()
    loads[4].wait()
    bias[...] = jnp.where(iota((8, PMAX), 1) < plen_ref[0], 0.0, MASKED)
    spread = iota((256, 128), 0) % (RANKS * ROWS) == iota((256, 128), 1)

    def prefix(n, carry):
        group = lax.rem(n + last, GROUPS)
        arrived(q_got, q_rsem, group, RANKS)
        rows = q_got[pl.ds(group * PAIR, PAIR)].reshape(256, HD)
        scores = scores_of(rows, kc[...]) + bias[0:1, :]
        averages, logs = softmax_values(scores, vc[...])
        m_out[pl.ds(group * PAIR, PAIR)] = averages.astype(jnp.bfloat16).reshape(PAIR, ROWS, HD)
        packed = jnp.where(spread, logs, 0.0).reshape(NX, RANKS * ROWS, HD)
        l_out[pl.ds(group * NX, NX)] = jnp.sum(packed, axis=1, keepdims=True)
        send(m_out, m_got, m_ssem, m_rsem, group, RANKS, False)
        send(l_out, l_got, l_ssem, l_rsem, group, 1, False)
        return carry

    lax.fori_loop(0, GROUPS, prefix, 0)

    loads[5].wait()
    acc[...] = jnp.zeros_like(acc)
    slot_lane8 = iota((LENGTH, 128), 1)

    def finish(n, carry):
        group = lax.rem(n + last, GROUPS)
        arrived(m_got, m_rsem, group, RANKS)
        arrived(l_got, l_rsem, group, 1)
        logs = jnp.broadcast_to(l_got[pl.ds(group * NX, NX)], (NX, RANKS * ROWS, HD))
        logs = jnp.where(spread, logs.reshape(256, HD), 0.0)
        logs = jnp.sum(logs, axis=1, keepdims=True).reshape(PAIR, ROWS, 1)
        squares, dots = acc[0], acc[1]
        for n in range(PAIR):
            slot = group * PAIR + n
            cand = idx_s[0, slot]
            far_log = jnp.broadcast_to(logs[n], (ROWS, HD))
            near_log = own_l[cand]
            top = jnp.maximum(far_log, near_log)
            far, near = jnp.exp2(far_log - top), jnp.exp2(near_log - top)
            mixed = (far * m_got[slot].astype(jnp.float32) + near * own_o[cand]) / (far + near)
            stream = res[cand].astype(jnp.float32)
            square = jnp.zeros((LENGTH, HD), jnp.float32)
            dot = jnp.zeros((LENGTH, HD), jnp.float32)
            for head in range(HEADS):
                hidden = (
                    stream[:, head * HD : (head + 1) * HD]
                    + mixed[head * LENGTH : (head + 1) * LENGTH]
                )
                square += hidden * hidden
                dot += hidden * weight_ref[head : head + 1, :]
            here = slot_lane8 == slot
            squares += jnp.where(here, jnp.sum(square, axis=1, keepdims=True), 0.0)
            dots += jnp.where(here, jnp.sum(dot, axis=1, keepdims=True), 0.0)
        acc[0], acc[1] = squares, dots
        return carry

    lax.fori_loop(0, GROUPS, finish, 0)

    part[my_t] = acc[...]
    shares = []
    for offset in range(1, NT):
        shares.append(
            pltpu.make_async_remote_copy(
                src_ref=acc,
                dst_ref=part.at[my_t],
                send_sem=p_ssem.at[offset],
                recv_sem=p_rsem.at[offset],
                device_id={"tensor": lax.rem(my_t + offset, NT)},
                device_id_type=MESH,
            )
        )
        shares[-1].start()
    for share in shares:
        share.wait_recv()
    total = part[0]
    for n in range(1, NT):
        total += part[n]
    scored = total[1] * lax.rsqrt(total[0] / FEATURES + EPSILON)
    result = jnp.zeros((LENGTH, 128), jnp.float32)
    for _ in range(3):
        piece = scored.astype(jnp.bfloat16)
        scored = scored - piece.astype(jnp.float32)
        result += jnp.dot(piece, place[...], preferred_element_type=jnp.float32)
    inside = iota((LENGTH, 128), 0) < len_ref[...]
    out_ref[...] = jnp.where(inside, result, 0.0)[:, :CANDS]

    for share in shares:
        share.wait_send()

    def sent(source, ssem, group, per, blocks):
        whole = source.at[pl.ds(group * NX * per, blocks * per)]
        pltpu.make_async_copy(whole, whole, ssem.at[group]).wait()

    def drain(group, carry):
        sent(q_out, q_ssem, group, RANKS, NX)
        sent(m_out, m_ssem, group, RANKS, NX)
        sent(l_out, l_ssem, group, 1, NX)
        return carry

    lax.fori_loop(0, last, drain, 0)
    sent(q_out, q_ssem, last, RANKS, NX - 1)
    sent(m_out, m_ssem, last, RANKS, NX - 1)
    sent(l_out, l_ssem, last, 1, NX - 1)


def body(
    queries,
    keys_new,
    values_new,
    residual,
    cand_len,
    owner_map,
    prompt_len,
    keys_cache,
    values_cache,
    norm_gain,
    value_head,
):
    bf16, f32 = jnp.bfloat16, jnp.float32
    weight = (norm_gain.astype(f32) * value_head.astype(f32)).reshape(HEADS, HD)
    vmem = pl.BlockSpec(memory_space=pltpu.VMEM)
    hbm = pl.BlockSpec(memory_space=pl.ANY)
    slots = pltpu.VMEM((SLOTS, ROWS, HD), bf16)
    logs = pltpu.VMEM((GROUPS * NX, 1, HD), f32)
    by_group = pltpu.SemaphoreType.DMA((GROUPS,))
    by_offset = pltpu.SemaphoreType.DMA((NT,))
    scored = pl.pallas_call(
        kernel,
        out_shape=jax.ShapeDtypeStruct((LENGTH, CANDS), f32),
        in_specs=[vmem, vmem, vmem, pl.BlockSpec(memory_space=pltpu.SMEM)] + [hbm] * 6,
        out_specs=vmem,
        scratch_shapes=[
            pltpu.VMEM((CANDS, ROWS, HD), bf16),
            pltpu.VMEM((CANDS * LENGTH, HD), bf16),
            pltpu.VMEM((CANDS * LENGTH, HD), bf16),
            pltpu.VMEM((CANDS, LENGTH, HEADS * HD), bf16),
            pltpu.VMEM((PMAX, HD), bf16),
            pltpu.VMEM((PMAX, HD), bf16),
            pltpu.VMEM((CANDS, ROWS, HD), bf16),
            slots,
            slots,
            slots,
            slots,
            logs,
            logs,
            pltpu.VMEM((CANDS, ROWS, HD), f32),
            pltpu.VMEM((CANDS, ROWS, HD), f32),
            pltpu.VMEM((8, PMAX), f32),
            pltpu.VMEM((8, 128), jnp.int32),
            pltpu.SMEM((8, 128), jnp.int32),
            pltpu.VMEM((128, 128), bf16),
            pltpu.VMEM((2, LENGTH, 128), f32),
            pltpu.VMEM((NT, 2, LENGTH, 128), f32),
            pltpu.SemaphoreType.DMA((6,)),
            pltpu.SemaphoreType.DMA,
            by_group,
            by_group,
            by_group,
            by_group,
            by_group,
            by_group,
            by_offset,
            by_offset,
        ],
        compiler_params=pltpu.CompilerParams(
            collective_id=0, has_side_effects=True, vmem_limit_bytes=40 * 2**20
        ),
    )(
        jnp.pad(owner_map, (0, 128 - CANDS)).reshape(1, 128),
        jnp.pad(cand_len, (0, 128 - CANDS)).reshape(1, 128),
        weight,
        prompt_len,
        queries.reshape(CANDS, ROWS, HD),
        keys_new.reshape(CANDS * LENGTH, HD),
        values_new.reshape(CANDS * LENGTH, HD),
        residual,
        keys_cache.reshape(PMAX, HD),
        values_cache.reshape(PMAX, HD),
    )
    return scored.T


def solution(mesh):
    in_specs = (
        P("dp", None, "tensor", None),
        P("dp", None, "tensor", None),
        P("dp", None, "tensor", None),
        P("dp", None, "tensor"),
        P("dp"),
        P("dp"),
        P("dp"),
        P("dp", None, "tensor", None),
        P("dp", None, "tensor", None),
        P("tensor"),
        P("tensor"),
    )
    out_specs = P("dp", None)
    return jax.shard_map(body, mesh=mesh, in_specs=in_specs, out_specs=out_specs, check_vma=False)
```

```python
import functools
import math

import jax
import jax.numpy as jnp
from jax import lax
from jax.experimental import pallas as pl
from jax.experimental.pallas import tpu as pltpu
from jax.sharding import PartitionSpec as P

EPSILON = 1e-05
MESH = pl.DeviceIdType.MESH
NZ = 16
NX = 4
NT = 8
RANKS = 2
HALF = NZ // 2
LEAD = 4
GROUPS = NZ
PAIR = NX * RANKS
SLOTS = GROUPS * PAIR
LENGTH = 8
HEADS = 4
ROWS = HEADS * LENGTH
HD = 128
PMAX = 2048
CANDS = 64
FEATURES = 4096
MASKED = -1e30
LOG2E = math.log2(math.e)


def iota(shape, dim):
    return lax.broadcasted_iota(jnp.int32, shape, dim)


def send_order(step):
    return jnp.where(lax.rem(step, 2) == 0, HALF - step // 2, lax.rem(NZ - step // 2, NZ))


def source_of(step, z):
    middle = step - LEAD
    later = jnp.where(step < LEAD, 0, jnp.where(step < GROUPS - LEAD, lax.rem(middle + GROUPS, 2), 1))
    turn = jnp.where(later == 0, LEAD + middle // 2, middle // 2)
    turn = jnp.where(step < LEAD, step, jnp.where(step < GROUPS - LEAD, turn, step - HALF))
    return later * HALF + lax.rem(z + turn, HALF)


def kernel(
    plen_ref,
    owner_hbm,
    len_hbm,
    gain_hbm,
    head_hbm,
    q_hbm,
    kn_hbm,
    vn_hbm,
    res_hbm,
    kc_hbm,
    vc_hbm,
    out_ref,
    owner_ref,
    len_ref,
    gain_ref,
    head_ref,
    q_in,
    kn,
    vn,
    res,
    kc,
    vc,
    q_perm,
    q_out,
    q_got,
    m_out,
    m_got,
    l_out,
    l_got,
    own_o,
    own_l,
    bias,
    idx_v,
    idx_s,
    place,
    acc,
    part,
    load_sem,
    idx_sem,
    q_ssem,
    q_rsem,
    m_ssem,
    m_rsem,
    l_ssem,
    l_rsem,
    p_ssem,
    p_rsem,
):
    me = lax.axis_index("dp")
    my_t = lax.axis_index("tensor")
    my_z, my_x = lax.div(me, NX), lax.rem(me, NX)

    def partner(dz, dx):
        return lax.rem(my_z + dz, NZ) * NX + lax.rem(my_x + dx, NX)

    loads = [
        pltpu.make_async_copy(source, target, load_sem.at[n])
        for n, (source, target) in enumerate(
            [
                (owner_hbm, owner_ref),
                (q_hbm, q_in),
                (kn_hbm, kn),
                (vn_hbm, vn),
                (kc_hbm, kc),
                (vc_hbm, vc),
                (res_hbm, res),
                (len_hbm, len_ref),
                (gain_hbm, gain_ref),
                (head_hbm, head_ref),
            ]
        )
    ]
    for load in loads:
        load.start()

    barrier = pltpu.get_barrier_semaphore()

    def greet(offset, carry):
        other = lax.rem(me + offset, NZ * NX)
        pl.semaphore_signal(barrier, inc=1, device_id={"dp": other}, device_id_type=MESH)
        return carry

    lax.fori_loop(1, NZ * NX, greet, 0)
    for offset in range(1, NT):
        pl.semaphore_signal(
            barrier,
            inc=1,
            device_id={"tensor": lax.rem(my_t + offset, NT)},
            device_id_type=MESH,
        )

    loads[0].wait()
    lane = iota((CANDS, CANDS), 1)
    row = iota((CANDS, CANDS), 0)
    owner = jnp.broadcast_to(owner_ref[...], (CANDS, CANDS))
    dz = lax.rem(lax.div(owner, NX) - my_z + NZ, NZ)
    dx = lax.rem(lax.rem(owner, NX) - my_x + NX, NX)
    pair_lane = dz * NX + dx
    pair_row = pair_lane.T
    same = pair_lane == pair_row
    rank_lane = jnp.sum(jnp.where(same & (row < lane), 1, 0), axis=0, keepdims=True)
    rank_row = jnp.sum(jnp.where(same & (lane < row), 1, 0), axis=1, keepdims=True)
    slot_lane = pair_lane[0:1] * RANKS + rank_lane
    slot_row = pair_row[:, 0:1] * RANKS + rank_row
    place[...] = jnp.where(iota((SLOTS, CANDS), 0) == slot_lane, 1.0, 0.0).astype(jnp.bfloat16)
    held = jnp.where(slot_row == iota((CANDS, SLOTS), 1), iota((CANDS, SLOTS), 0), 0)
    chosen = jnp.sum(held, axis=0, keepdims=True)
    idx_v[...] = jnp.broadcast_to(chosen, (8, 128))
    fetch = pltpu.make_async_copy(idx_v, idx_s, idx_sem)
    fetch.start()

    to_row = iota((256, 256), 0)
    from_row = iota((256, 256), 1)
    source_row = (to_row // ROWS) * ROWS + (to_row % LENGTH) * HEADS + (to_row % ROWS) // LENGTH
    shuffle = jnp.where(from_row == source_row, 1.0, 0.0).astype(jnp.bfloat16)
    loads[1].wait()

    def reorder(n, carry):
        rows = q_in[pl.ds(n * 8, 8)].reshape(256, HD)
        mixed = jnp.dot(shuffle, rows, preferred_element_type=jnp.float32)
        q_perm[pl.ds(n * 8, 8)] = mixed.astype(jnp.bfloat16).reshape(8, ROWS, HD)
        return carry

    lax.fori_loop(0, CANDS // 8, reorder, 0)
    fetch.wait()

    pl.semaphore_wait(barrier, NZ * NX - 1 + NT - 1)

    def span(ref, group, dx, per):
        return ref.at[pl.ds((group * NX + dx) * per, per)]

    def remote(source, target, ssem, rsem, group, dx, per, forth):
        to = partner(group, dx) if forth else partner(NZ - group, NX - dx)
        return pltpu.make_async_remote_copy(
            src_ref=span(source, group, dx, per),
            dst_ref=span(target, group, dx, per),
            send_sem=ssem.at[group],
            recv_sem=rsem.at[group],
            device_id={"dp": to},
            device_id_type=MESH,
        )

    def keep(source, target, rsem, per):
        return pltpu.make_async_copy(
            span(source, 0, 0, per), span(target, 0, 0, per), rsem.at[0]
        )

    def send(source, target, ssem, rsem, group, per, forth):
        for dx in range(1, NX):
            remote(source, target, ssem, rsem, group, dx, per, forth).start()

        @pl.when(group != 0)
        def _():
            remote(source, target, ssem, rsem, group, 0, per, forth).start()

        @pl.when(group == 0)
        def _():
            keep(source, target, rsem, per).start()

    def arrived(target, rsem, group, per):
        whole = target.at[pl.ds(group * NX * per, NX * per)]
        pltpu.make_async_copy(whole, whole, rsem.at[group]).wait()

    def send_query(group):
        for n in range(PAIR):
            slot = group * PAIR + n
            q_out[slot] = q_perm[idx_s[0, slot]]
        send(q_out, q_got, q_ssem, q_rsem, group, RANKS, True)

    def send_first(step, carry):
        send_query(send_order(step))
        return carry

    lax.fori_loop(0, GROUPS, send_first, 0)

    scale = LOG2E / math.sqrt(HD)

    def softmax_values(scores, value_rows):
        highest = jnp.max(scores, axis=1, keepdims=True)
        powers = jnp.exp2(scores - highest)
        total = jnp.sum(powers, axis=1, keepdims=True)
        sums = jnp.dot(powers.astype(jnp.bfloat16), value_rows, preferred_element_type=jnp.float32)
        return sums / total, highest + jnp.log2(total)

    def scores_of(query_rows, key_rows):
        return (
            lax.dot_general(
                query_rows, key_rows, (((1,), (1,)), ((), ())), preferred_element_type=jnp.float32
            )
            * scale
        )

    loads[2].wait()
    loads[3].wait()
    at_row = iota((512, 128), 0)
    at_key = iota((512, 128), 1)
    seen = (at_row // ROWS == at_key // LENGTH) & (at_key % LENGTH <= at_row % LENGTH)

    def own_tokens(n, carry):
        rows = q_perm[pl.ds(n * 16, 16)].reshape(512, HD)
        scores = scores_of(rows, kn[pl.ds(n * 128, 128)])
        scores = jnp.where(seen, scores, MASKED)
        averages, logs = softmax_values(scores, vn[pl.ds(n * 128, 128)])
        own_o[pl.ds(n * 16, 16)] = averages.reshape(16, ROWS, HD)
        own_l[pl.ds(n * 16, 16)] = jnp.broadcast_to(logs, (512, HD)).reshape(16, ROWS, HD)
        return carry

    lax.fori_loop(0, CANDS // 16, own_tokens, 0)

    loads[4].wait()
    loads[5].wait()
    bias[...] = jnp.where(iota((8, PMAX), 1) < plen_ref[0], 0.0, MASKED)
    spread = iota((256, 128), 0) % (RANKS * ROWS) == iota((256, 128), 1)

    def prefix(step, carry):
        group = lax.rem(my_z - source_of(step, my_z) + NZ, NZ)
        arrived(q_got, q_rsem, group, RANKS)
        rows = q_got[pl.ds(group * PAIR, PAIR)].reshape(256, HD)
        scores = scores_of(rows, kc[...]) + bias[0:1, :]
        averages, logs = softmax_values(scores, vc[...])
        m_out[pl.ds(group * PAIR, PAIR)] = averages.astype(jnp.bfloat16).reshape(PAIR, ROWS, HD)
        packed = jnp.where(spread, logs, 0.0).reshape(NX, RANKS * ROWS, HD)
        l_out[pl.ds(group * NX, NX)] = jnp.sum(packed, axis=1, keepdims=True)
        send(m_out, m_got, m_ssem, m_rsem, group, RANKS, False)
        send(l_out, l_got, l_ssem, l_rsem, group, 1, False)
        return carry

    lax.fori_loop(0, GROUPS, prefix, 0)

    for load in loads[6:]:
        load.wait()
    weight = gain_ref[...].astype(jnp.float32) * head_ref[...].astype(jnp.float32)
    acc[...] = jnp.zeros_like(acc)
    slot_lane8 = iota((LENGTH, 128), 1)

    def finish(step, carry):
        group = send_order(step)
        arrived(m_got, m_rsem, group, RANKS)
        arrived(l_got, l_rsem, group, 1)
        logs = jnp.broadcast_to(l_got[pl.ds(group * NX, NX)], (NX, RANKS * ROWS, HD))
        logs = jnp.where(spread, logs.reshape(256, HD), 0.0)
        logs = jnp.sum(logs, axis=1, keepdims=True).reshape(PAIR, ROWS, 1)
        squares, dots = acc[0], acc[1]
        for n in range(PAIR):
            slot = group * PAIR + n
            cand = idx_s[0, slot]
            far_log = jnp.broadcast_to(logs[n], (ROWS, HD))
            near_log = own_l[cand]
            top = jnp.maximum(far_log, near_log)
            far, near = jnp.exp2(far_log - top), jnp.exp2(near_log - top)
            mixed = (far * m_got[slot].astype(jnp.float32) + near * own_o[cand]) / (far + near)
            stream = res[cand].astype(jnp.float32)
            square = jnp.zeros((LENGTH, HD), jnp.float32)
            dot = jnp.zeros((LENGTH, HD), jnp.float32)
            for head in range(HEADS):
                hidden = (
                    stream[:, head * HD : (head + 1) * HD]
                    + mixed[head * LENGTH : (head + 1) * LENGTH]
                )
                square += hidden * hidden
                dot += hidden * weight[head : head + 1, :]
            here = slot_lane8 == slot
            squares += jnp.where(here, jnp.sum(square, axis=1, keepdims=True), 0.0)
            dots += jnp.where(here, jnp.sum(dot, axis=1, keepdims=True), 0.0)
        acc[0], acc[1] = squares, dots
        return carry

    lax.fori_loop(0, GROUPS, finish, 0)

    part[my_t] = acc[...]
    shares = []
    for offset in range(1, NT):
        shares.append(
            pltpu.make_async_remote_copy(
                src_ref=acc,
                dst_ref=part.at[my_t],
                send_sem=p_ssem.at[offset],
                recv_sem=p_rsem.at[offset],
                device_id={"tensor": lax.rem(my_t + offset, NT)},
                device_id_type=MESH,
            )
        )
        shares[-1].start()
    for share in shares:
        share.wait_recv()
    total = part[0]
    for n in range(1, NT):
        total += part[n]
    scored = total[1] * lax.rsqrt(total[0] / FEATURES + EPSILON)
    result = jnp.zeros((LENGTH, CANDS), jnp.float32)
    for _ in range(3):
        piece = scored.astype(jnp.bfloat16)
        scored = scored - piece.astype(jnp.float32)
        result += jnp.dot(piece, place[...], preferred_element_type=jnp.float32)
    inside = iota((LENGTH, CANDS), 0) < len_ref[...]
    out_ref[...] = jnp.where(inside, result, 0.0)

    for share in shares:
        share.wait_send()

    def sent(source, ssem, group, per, blocks):
        whole = source.at[pl.ds(group * NX * per, blocks * per)]
        pltpu.make_async_copy(whole, whole, ssem.at[group]).wait()

    def drain(group, carry):
        sent(q_out, q_ssem, group, RANKS, NX)
        sent(m_out, m_ssem, group, RANKS, NX)
        sent(l_out, l_ssem, group, 1, NX)
        return carry

    lax.fori_loop(1, GROUPS, drain, 0)
    sent(q_out, q_ssem, 0, RANKS, NX - 1)
    sent(m_out, m_ssem, 0, RANKS, NX - 1)
    sent(l_out, l_ssem, 0, 1, NX - 1)


def body(
    queries,
    keys_new,
    values_new,
    residual,
    cand_len,
    owner_map,
    prompt_len,
    keys_cache,
    values_cache,
    norm_gain,
    value_head,
):
    bf16, f32 = jnp.bfloat16, jnp.float32
    vmem = pl.BlockSpec(memory_space=pltpu.VMEM)
    hbm = pl.BlockSpec(memory_space=pl.ANY)
    slots = pltpu.VMEM((SLOTS, ROWS, HD), bf16)
    logs = pltpu.VMEM((GROUPS * NX, 1, HD), f32)
    by_group = pltpu.SemaphoreType.DMA((GROUPS,))
    by_offset = pltpu.SemaphoreType.DMA((NT,))
    scored = pl.pallas_call(
        kernel,
        out_shape=jax.ShapeDtypeStruct((LENGTH, CANDS), f32),
        in_specs=[pl.BlockSpec(memory_space=pltpu.SMEM)] + [hbm] * 10,
        out_specs=vmem,
        scratch_shapes=[
            pltpu.VMEM((1, CANDS), jnp.int32),
            pltpu.VMEM((1, CANDS), jnp.int32),
            pltpu.VMEM((HEADS, HD), bf16),
            pltpu.VMEM((HEADS, HD), bf16),
            pltpu.VMEM((CANDS, ROWS, HD), bf16),
            pltpu.VMEM((CANDS * LENGTH, HD), bf16),
            pltpu.VMEM((CANDS * LENGTH, HD), bf16),
            pltpu.VMEM((CANDS, LENGTH, HEADS * HD), bf16),
            pltpu.VMEM((PMAX, HD), bf16),
            pltpu.VMEM((PMAX, HD), bf16),
            pltpu.VMEM((CANDS, ROWS, HD), bf16),
            slots,
            slots,
            slots,
            slots,
            logs,
            logs,
            pltpu.VMEM((CANDS, ROWS, HD), f32),
            pltpu.VMEM((CANDS, ROWS, HD), f32),
            pltpu.VMEM((8, PMAX), f32),
            pltpu.VMEM((8, 128), jnp.int32),
            pltpu.SMEM((8, 128), jnp.int32),
            pltpu.VMEM((SLOTS, CANDS), bf16),
            pltpu.VMEM((2, LENGTH, 128), f32),
            pltpu.VMEM((NT, 2, LENGTH, 128), f32),
            pltpu.SemaphoreType.DMA((10,)),
            pltpu.SemaphoreType.DMA,
            by_group,
            by_group,
            by_group,
            by_group,
            by_group,
            by_group,
            by_offset,
            by_offset,
        ],
        compiler_params=pltpu.CompilerParams(
            collective_id=0, has_side_effects=True, vmem_limit_bytes=62 * 2**20
        ),
    )(
        prompt_len,
        owner_map.reshape(1, CANDS),
        cand_len.reshape(1, CANDS),
        norm_gain.reshape(HEADS, HD),
        value_head.reshape(HEADS, HD),
        queries.reshape(CANDS, ROWS, HD),
        keys_new.reshape(CANDS * LENGTH, HD),
        values_new.reshape(CANDS * LENGTH, HD),
        residual,
        keys_cache.reshape(PMAX, HD),
        values_cache.reshape(PMAX, HD),
    )
    return scored.T


def solution(mesh):
    in_specs = (
        P("dp", None, "tensor", None),
        P("dp", None, "tensor", None),
        P("dp", None, "tensor", None),
        P("dp", None, "tensor"),
        P("dp"),
        P("dp"),
        P("dp"),
        P("dp", None, "tensor", None),
        P("dp", None, "tensor", None),
        P("tensor"),
        P("tensor"),
    )
    out_specs = P("dp", None)
    return jax.shard_map(body, mesh=mesh, in_specs=in_specs, out_specs=out_specs, check_vma=False)
```

```python
import functools
import math

import jax
import jax.numpy as jnp
from jax import lax
from jax.experimental import pallas as pl
from jax.experimental.pallas import tpu as pltpu
from jax.sharding import PartitionSpec as P

EPSILON = 1e-05
MESH = pl.DeviceIdType.MESH
NZ = 16
NX = 4
NT = 8
RANKS = 2
HALF = NZ // 2
LEAD = 4
GROUPS = NZ
PAIR = NX * RANKS
SLOTS = GROUPS * PAIR
LENGTH = 8
HEADS = 4
ROWS = HEADS * LENGTH
HD = 128
PMAX = 2048
CANDS = 64
FEATURES = 4096
MASKED = -1e30
LOG2E = math.log2(math.e)


def iota(shape, dim):
    return lax.broadcasted_iota(jnp.int32, shape, dim)


def send_order(step):
    return jnp.where(lax.rem(step, 2) == 0, HALF - step // 2, lax.rem(NZ - step // 2, NZ))


def source_of(step, z):
    middle = step - LEAD
    later = jnp.where(step < LEAD, 0, jnp.where(step < GROUPS - LEAD, lax.rem(middle + GROUPS, 2), 1))
    turn = jnp.where(later == 0, LEAD + middle // 2, middle // 2)
    turn = jnp.where(step < LEAD, step, jnp.where(step < GROUPS - LEAD, turn, step - HALF))
    return later * HALF + lax.rem(z + turn, HALF)


def kernel(
    plen_ref,
    owner_hbm,
    len_hbm,
    gain_hbm,
    head_hbm,
    q_hbm,
    kn_hbm,
    vn_hbm,
    res_hbm,
    kc_hbm,
    vc_hbm,
    out_ref,
    owner_ref,
    len_ref,
    gain_ref,
    head_ref,
    q_in,
    kn,
    vn,
    res,
    kc,
    vc,
    q_perm,
    q_out,
    q_got,
    m_out,
    m_got,
    l_out,
    l_got,
    own_o,
    own_l,
    bias,
    idx_v,
    idx_s,
    place,
    acc,
    part,
    load_sem,
    idx_sem,
    q_ssem,
    q_rsem,
    m_ssem,
    m_rsem,
    l_ssem,
    l_rsem,
    p_ssem,
    p_rsem,
):
    me = lax.axis_index("dp")
    my_t = lax.axis_index("tensor")
    my_z, my_x = lax.div(me, NX), lax.rem(me, NX)

    def partner(dz, dx):
        return lax.rem(my_z + dz, NZ) * NX + lax.rem(my_x + dx, NX)

    loads = [
        pltpu.make_async_copy(source, target, load_sem.at[n])
        for n, (source, target) in enumerate(
            [
                (owner_hbm, owner_ref),
                (q_hbm, q_in),
                (kn_hbm, kn),
                (vn_hbm, vn),
                (kc_hbm, kc),
                (vc_hbm, vc),
                (res_hbm, res),
                (len_hbm, len_ref),
                (gain_hbm, gain_ref),
                (head_hbm, head_ref),
            ]
        )
    ]
    for load in loads:
        load.start()

    barrier = pltpu.get_barrier_semaphore()

    def greet(offset, carry):
        other = lax.rem(me + offset, NZ * NX)
        pl.semaphore_signal(barrier, inc=1, device_id={"dp": other}, device_id_type=MESH)
        return carry

    lax.fori_loop(1, NZ * NX, greet, 0)
    for offset in range(1, NT):
        pl.semaphore_signal(
            barrier,
            inc=1,
            device_id={"tensor": lax.rem(my_t + offset, NT)},
            device_id_type=MESH,
        )

    loads[0].wait()
    lane = iota((CANDS, CANDS), 1)
    row = iota((CANDS, CANDS), 0)
    owner = jnp.broadcast_to(owner_ref[...], (CANDS, CANDS))
    dz = lax.rem(lax.div(owner, NX) - my_z + NZ, NZ)
    dx = lax.rem(lax.rem(owner, NX) - my_x + NX, NX)
    pair_lane = dz * NX + dx
    pair_row = pair_lane.T
    same = pair_lane == pair_row
    rank_lane = jnp.sum(jnp.where(same & (row < lane), 1, 0), axis=0, keepdims=True)
    rank_row = jnp.sum(jnp.where(same & (lane < row), 1, 0), axis=1, keepdims=True)
    slot_lane = pair_lane[0:1] * RANKS + rank_lane
    slot_row = pair_row[:, 0:1] * RANKS + rank_row
    place[...] = jnp.where(iota((SLOTS, CANDS), 0) == slot_lane, 1.0, 0.0).astype(jnp.bfloat16)
    held = jnp.where(slot_row == iota((CANDS, SLOTS), 1), iota((CANDS, SLOTS), 0), 0)
    chosen = jnp.sum(held, axis=0, keepdims=True)
    idx_v[...] = jnp.broadcast_to(chosen, (8, 128))
    fetch = pltpu.make_async_copy(idx_v, idx_s, idx_sem)
    fetch.start()

    to_row = iota((256, 256), 0)
    from_row = iota((256, 256), 1)
    source_row = (to_row // ROWS) * ROWS + (to_row % LENGTH) * HEADS + (to_row % ROWS) // LENGTH
    shuffle = jnp.where(from_row == source_row, 1.0, 0.0).astype(jnp.bfloat16)
    loads[1].wait()

    def reorder(n, carry):
        rows = q_in[pl.ds(n * 8, 8)].reshape(256, HD)
        mixed = jnp.dot(shuffle, rows, preferred_element_type=jnp.float32)
        q_perm[pl.ds(n * 8, 8)] = mixed.astype(jnp.bfloat16).reshape(8, ROWS, HD)
        return carry

    lax.fori_loop(0, CANDS // 8, reorder, 0)
    fetch.wait()

    pl.semaphore_wait(barrier, NZ * NX - 1 + NT - 1)

    def span(ref, group, dx, per):
        return ref.at[pl.ds((group * NX + dx) * per, per)]

    def remote(source, target, ssem, rsem, group, dx, per, forth):
        to = partner(group, dx) if forth else partner(NZ - group, NX - dx)
        return pltpu.make_async_remote_copy(
            src_ref=span(source, group, dx, per),
            dst_ref=span(target, group, dx, per),
            send_sem=ssem.at[group],
            recv_sem=rsem.at[group],
            device_id={"dp": to},
            device_id_type=MESH,
        )

    def keep(source, target, rsem, per):
        return pltpu.make_async_copy(
            span(source, 0, 0, per), span(target, 0, 0, per), rsem.at[0]
        )

    def send(source, target, ssem, rsem, group, per, forth):
        for dx in range(1, NX):
            remote(source, target, ssem, rsem, group, dx, per, forth).start()

        @pl.when(group != 0)
        def _():
            remote(source, target, ssem, rsem, group, 0, per, forth).start()

        @pl.when(group == 0)
        def _():
            keep(source, target, rsem, per).start()

    def arrived(target, rsem, group, per):
        whole = target.at[pl.ds(group * NX * per, NX * per)]
        pltpu.make_async_copy(whole, whole, rsem.at[group]).wait()

    def sent(source, ssem, group, per, blocks):
        whole = source.at[pl.ds(group * NX * per, blocks * per)]
        pltpu.make_async_copy(whole, whole, ssem.at[group]).wait()

    def send_query(group):
        for n in range(PAIR):
            slot = group * PAIR + n
            q_out[slot] = q_perm[idx_s[0, slot]]
        send(q_out, q_got, q_ssem, q_rsem, group, RANKS, True)

    def send_first(step, carry):
        send_query(send_order(step))
        return carry

    lax.fori_loop(0, GROUPS, send_first, 0)

    scale = LOG2E / math.sqrt(HD)

    def softmax_values(scores, value_rows):
        highest = jnp.max(scores, axis=1, keepdims=True)
        powers = jnp.exp2(scores - highest)
        total = jnp.sum(powers, axis=1, keepdims=True)
        sums = jnp.dot(powers.astype(jnp.bfloat16), value_rows, preferred_element_type=jnp.float32)
        return sums / total, highest + jnp.log2(total)

    def scores_of(query_rows, key_rows):
        return (
            lax.dot_general(
                query_rows, key_rows, (((1,), (1,)), ((), ())), preferred_element_type=jnp.float32
            )
            * scale
        )

    loads[2].wait()
    loads[3].wait()
    at_row = iota((512, 128), 0)
    at_key = iota((512, 128), 1)
    seen = (at_row // ROWS == at_key // LENGTH) & (at_key % LENGTH <= at_row % LENGTH)

    def own_tokens(n, carry):
        rows = q_perm[pl.ds(n * 16, 16)].reshape(512, HD)
        scores = scores_of(rows, kn[pl.ds(n * 128, 128)])
        scores = jnp.where(seen, scores, MASKED)
        averages, logs = softmax_values(scores, vn[pl.ds(n * 128, 128)])
        own_o[pl.ds(n * 16, 16)] = averages.reshape(16, ROWS, HD)
        own_l[pl.ds(n * 16, 16)] = jnp.broadcast_to(logs, (512, HD)).reshape(16, ROWS, HD)
        return carry

    lax.fori_loop(0, CANDS // 16, own_tokens, 0)

    loads[4].wait()
    loads[5].wait()
    bias[...] = jnp.where(iota((8, PMAX), 1) < plen_ref[0], 0.0, MASKED)
    spread = iota((256, 128), 0) % (RANKS * ROWS) == iota((256, 128), 1)

    def prefix(step, carry):
        group = lax.rem(my_z - source_of(step, my_z) + NZ, NZ)
        arrived(q_got, q_rsem, group, RANKS)
        rows = q_got[pl.ds(group * PAIR, PAIR)].reshape(256, HD)
        scores = scores_of(rows, kc[...]) + bias[0:1, :]
        averages, logs = softmax_values(scores, vc[...])
        m_out[pl.ds(group * PAIR, PAIR)] = averages.astype(jnp.bfloat16).reshape(PAIR, ROWS, HD)
        packed = jnp.where(spread, logs, 0.0).reshape(NX, RANKS * ROWS, HD)
        l_out[pl.ds(group * NX, NX)] = jnp.sum(packed, axis=1, keepdims=True)
        send(m_out, m_got, m_ssem, m_rsem, group, RANKS, False)
        send(l_out, l_got, l_ssem, l_rsem, group, 1, False)
        return carry

    lax.fori_loop(0, GROUPS, prefix, 0)

    def drain_queries(group, carry):
        sent(q_out, q_ssem, group, RANKS, NX)
        return carry

    lax.fori_loop(1, GROUPS, drain_queries, 0)
    sent(q_out, q_ssem, 0, RANKS, NX - 1)

    for load in loads[6:]:
        load.wait()
    weight = gain_ref[...].astype(jnp.float32) * head_ref[...].astype(jnp.float32)
    acc[...] = jnp.zeros_like(acc)
    slot_lane8 = iota((LENGTH, 128), 1)

    def finish(step, carry):
        group = send_order(step)
        arrived(m_got, m_rsem, group, RANKS)
        arrived(l_got, l_rsem, group, 1)
        logs = jnp.broadcast_to(l_got[pl.ds(group * NX, NX)], (NX, RANKS * ROWS, HD))
        logs = jnp.where(spread, logs.reshape(256, HD), 0.0)
        logs = jnp.sum(logs, axis=1, keepdims=True).reshape(PAIR, ROWS, 1)
        squares, dots = acc[0], acc[1]
        for n in range(PAIR):
            slot = group * PAIR + n
            cand = idx_s[0, slot]
            far_log = jnp.broadcast_to(logs[n], (ROWS, HD))
            near_log = own_l[cand]
            top = jnp.maximum(far_log, near_log)
            far, near = jnp.exp2(far_log - top), jnp.exp2(near_log - top)
            mixed = (far * m_got[slot].astype(jnp.float32) + near * own_o[cand]) / (far + near)
            stream = res[cand].astype(jnp.float32)
            square = jnp.zeros((LENGTH, HD), jnp.float32)
            dot = jnp.zeros((LENGTH, HD), jnp.float32)
            for head in range(HEADS):
                hidden = (
                    stream[:, head * HD : (head + 1) * HD]
                    + mixed[head * LENGTH : (head + 1) * LENGTH]
                )
                square += hidden * hidden
                dot += hidden * weight[head : head + 1, :]
            here = slot_lane8 == slot
            squares += jnp.where(here, jnp.sum(square, axis=1, keepdims=True), 0.0)
            dots += jnp.where(here, jnp.sum(dot, axis=1, keepdims=True), 0.0)
        acc[0], acc[1] = squares, dots
        return carry

    lax.fori_loop(0, GROUPS, finish, 0)

    part[my_t] = acc[...]
    shares = []
    for offset in range(1, NT):
        shares.append(
            pltpu.make_async_remote_copy(
                src_ref=acc,
                dst_ref=part.at[my_t],
                send_sem=p_ssem.at[offset],
                recv_sem=p_rsem.at[offset],
                device_id={"tensor": lax.rem(my_t + offset, NT)},
                device_id_type=MESH,
            )
        )
        shares[-1].start()

    def drain(group, carry):
        sent(m_out, m_ssem, group, RANKS, NX)
        sent(l_out, l_ssem, group, 1, NX)
        return carry

    lax.fori_loop(1, GROUPS, drain, 0)
    sent(m_out, m_ssem, 0, RANKS, NX - 1)
    sent(l_out, l_ssem, 0, 1, NX - 1)

    for share in shares:
        share.wait_recv()
    total = part[0]
    for n in range(1, NT):
        total += part[n]
    scored = total[1] * lax.rsqrt(total[0] / FEATURES + EPSILON)
    result = jnp.zeros((LENGTH, CANDS), jnp.float32)
    for _ in range(3):
        piece = scored.astype(jnp.bfloat16)
        scored = scored - piece.astype(jnp.float32)
        result += jnp.dot(piece, place[...], preferred_element_type=jnp.float32)
    inside = iota((LENGTH, CANDS), 0) < len_ref[...]
    out_ref[...] = jnp.where(inside, result, 0.0)

    for share in shares:
        share.wait_send()


def body(
    queries,
    keys_new,
    values_new,
    residual,
    cand_len,
    owner_map,
    prompt_len,
    keys_cache,
    values_cache,
    norm_gain,
    value_head,
):
    bf16, f32 = jnp.bfloat16, jnp.float32
    vmem = pl.BlockSpec(memory_space=pltpu.VMEM)
    hbm = pl.BlockSpec(memory_space=pl.ANY)
    slots = pltpu.VMEM((SLOTS, ROWS, HD), bf16)
    logs = pltpu.VMEM((GROUPS * NX, 1, HD), f32)
    by_group = pltpu.SemaphoreType.DMA((GROUPS,))
    by_offset = pltpu.SemaphoreType.DMA((NT,))
    scored = pl.pallas_call(
        kernel,
        out_shape=jax.ShapeDtypeStruct((LENGTH, CANDS), f32),
        in_specs=[pl.BlockSpec(memory_space=pltpu.SMEM)] + [hbm] * 10,
        out_specs=vmem,
        scratch_shapes=[
            pltpu.VMEM((1, CANDS), jnp.int32),
            pltpu.VMEM((1, CANDS), jnp.int32),
            pltpu.VMEM((HEADS, HD), bf16),
            pltpu.VMEM((HEADS, HD), bf16),
            pltpu.VMEM((CANDS, ROWS, HD), bf16),
            pltpu.VMEM((CANDS * LENGTH, HD), bf16),
            pltpu.VMEM((CANDS * LENGTH, HD), bf16),
            pltpu.VMEM((CANDS, LENGTH, HEADS * HD), bf16),
            pltpu.VMEM((PMAX, HD), bf16),
            pltpu.VMEM((PMAX, HD), bf16),
            pltpu.VMEM((CANDS, ROWS, HD), bf16),
            slots,
            slots,
            slots,
            slots,
            logs,
            logs,
            pltpu.VMEM((CANDS, ROWS, HD), f32),
            pltpu.VMEM((CANDS, ROWS, HD), f32),
            pltpu.VMEM((8, PMAX), f32),
            pltpu.VMEM((8, 128), jnp.int32),
            pltpu.SMEM((8, 128), jnp.int32),
            pltpu.VMEM((SLOTS, CANDS), bf16),
            pltpu.VMEM((2, LENGTH, 128), f32),
            pltpu.VMEM((NT, 2, LENGTH, 128), f32),
            pltpu.SemaphoreType.DMA((10,)),
            pltpu.SemaphoreType.DMA,
            by_group,
            by_group,
            by_group,
            by_group,
            by_group,
            by_group,
            by_offset,
            by_offset,
        ],
        compiler_params=pltpu.CompilerParams(
            collective_id=0, has_side_effects=True, vmem_limit_bytes=62 * 2**20
        ),
    )(
        prompt_len,
        owner_map.reshape(1, CANDS),
        cand_len.reshape(1, CANDS),
        norm_gain.reshape(HEADS, HD),
        value_head.reshape(HEADS, HD),
        queries.reshape(CANDS, ROWS, HD),
        keys_new.reshape(CANDS * LENGTH, HD),
        values_new.reshape(CANDS * LENGTH, HD),
        residual,
        keys_cache.reshape(PMAX, HD),
        values_cache.reshape(PMAX, HD),
    )
    return scored.T


def solution(mesh):
    in_specs = (
        P("dp", None, "tensor", None),
        P("dp", None, "tensor", None),
        P("dp", None, "tensor", None),
        P("dp", None, "tensor"),
        P("dp"),
        P("dp"),
        P("dp"),
        P("dp", None, "tensor", None),
        P("dp", None, "tensor", None),
        P("tensor"),
        P("tensor"),
    )
    out_specs = P("dp", None)
    return jax.shard_map(body, mesh=mesh, in_specs=in_specs, out_specs=out_specs, check_vma=False)
```

```python
import functools
import math

import jax
import jax.numpy as jnp
from jax import lax
from jax.experimental import pallas as pl
from jax.experimental.pallas import tpu as pltpu
from jax.sharding import PartitionSpec as P

EPSILON = 1e-05
MESH = pl.DeviceIdType.MESH
NZ = 16
NX = 4
NT = 8
RANKS = 2
HALF = NZ // 2
LEAD = 4
GROUPS = NZ
PAIR = NX * RANKS
SLOTS = GROUPS * PAIR
LENGTH = 8
HEADS = 4
ROWS = HEADS * LENGTH
HD = 128
PMAX = 2048
CANDS = 64
FEATURES = 4096
MASKED = -1e30
LOG2E = math.log2(math.e)


def iota(shape, dim):
    return lax.broadcasted_iota(jnp.int32, shape, dim)


def send_order(step):
    return jnp.where(lax.rem(step, 2) == 0, HALF - step // 2, lax.rem(NZ - step // 2, NZ))


def source_of(step, z, way):
    middle = step - LEAD
    later = jnp.where(step < LEAD, 0, jnp.where(step < GROUPS - LEAD, lax.rem(middle + GROUPS, 2), 1))
    turn = jnp.where(later == 0, LEAD + middle // 2, middle // 2)
    turn = jnp.where(step < LEAD, step, jnp.where(step < GROUPS - LEAD, turn, step - HALF))
    return later * HALF + lax.rem(z + HALF + way * turn, HALF)


def kernel(
    plen_ref,
    owner_hbm,
    len_hbm,
    gain_hbm,
    head_hbm,
    q_hbm,
    kn_hbm,
    vn_hbm,
    res_hbm,
    kc_hbm,
    vc_hbm,
    out_ref,
    owner_ref,
    len_ref,
    gain_ref,
    head_ref,
    q_in,
    kn,
    vn,
    res,
    kc,
    vc,
    q_perm,
    q_out,
    q_got,
    m_out,
    m_got,
    l_out,
    l_got,
    own_o,
    own_l,
    bias,
    idx_v,
    idx_s,
    place,
    acc,
    part,
    load_sem,
    idx_sem,
    q_ssem,
    q_rsem,
    m_ssem,
    m_rsem,
    l_ssem,
    l_rsem,
    p_ssem,
    p_rsem,
):
    me = lax.axis_index("dp")
    my_t = lax.axis_index("tensor")
    my_z, my_x = lax.div(me, NX), lax.rem(me, NX)

    def partner(dz, dx):
        return lax.rem(my_z + dz, NZ) * NX + lax.rem(my_x + dx, NX)

    loads = [
        pltpu.make_async_copy(source, target, load_sem.at[n])
        for n, (source, target) in enumerate(
            [
                (owner_hbm, owner_ref),
                (q_hbm, q_in),
                (kn_hbm, kn),
                (vn_hbm, vn),
                (kc_hbm, kc),
                (vc_hbm, vc),
                (res_hbm, res),
                (len_hbm, len_ref),
                (gain_hbm, gain_ref),
                (head_hbm, head_ref),
            ]
        )
    ]
    for load in loads:
        load.start()

    barrier = pltpu.get_barrier_semaphore()

    def greet(offset, carry):
        other = lax.rem(me + offset, NZ * NX)
        pl.semaphore_signal(barrier, inc=1, device_id={"dp": other}, device_id_type=MESH)
        return carry

    lax.fori_loop(1, NZ * NX, greet, 0)
    for offset in range(1, NT):
        pl.semaphore_signal(
            barrier,
            inc=1,
            device_id={"tensor": lax.rem(my_t + offset, NT)},
            device_id_type=MESH,
        )

    loads[0].wait()
    lane = iota((CANDS, CANDS), 1)
    row = iota((CANDS, CANDS), 0)
    owner = jnp.broadcast_to(owner_ref[...], (CANDS, CANDS))
    dz = lax.rem(lax.div(owner, NX) - my_z + NZ, NZ)
    dx = lax.rem(lax.rem(owner, NX) - my_x + NX, NX)
    pair_lane = dz * NX + dx
    pair_row = pair_lane.T
    same = pair_lane == pair_row
    rank_lane = jnp.sum(jnp.where(same & (row < lane), 1, 0), axis=0, keepdims=True)
    rank_row = jnp.sum(jnp.where(same & (lane < row), 1, 0), axis=1, keepdims=True)
    slot_lane = pair_lane[0:1] * RANKS + rank_lane
    slot_row = pair_row[:, 0:1] * RANKS + rank_row
    place[...] = jnp.where(iota((SLOTS, CANDS), 0) == slot_lane, 1.0, 0.0).astype(jnp.bfloat16)
    held = jnp.where(slot_row == iota((CANDS, SLOTS), 1), iota((CANDS, SLOTS), 0), 0)
    chosen = jnp.sum(held, axis=0, keepdims=True)
    idx_v[...] = jnp.broadcast_to(chosen, (8, 128))
    fetch = pltpu.make_async_copy(idx_v, idx_s, idx_sem)
    fetch.start()

    to_row = iota((256, 256), 0)
    from_row = iota((256, 256), 1)
    source_row = (to_row // ROWS) * ROWS + (to_row % LENGTH) * HEADS + (to_row % ROWS) // LENGTH
    shuffle = jnp.where(from_row == source_row, 1.0, 0.0).astype(jnp.bfloat16)
    loads[1].wait()

    def reorder(n, carry):
        rows = q_in[pl.ds(n * 8, 8)].reshape(256, HD)
        mixed = jnp.dot(shuffle, rows, preferred_element_type=jnp.float32)
        q_perm[pl.ds(n * 8, 8)] = mixed.astype(jnp.bfloat16).reshape(8, ROWS, HD)
        return carry

    lax.fori_loop(0, CANDS // 8, reorder, 0)
    fetch.wait()

    pl.semaphore_wait(barrier, NZ * NX - 1 + NT - 1)

    def span(ref, group, dx, per):
        return ref.at[pl.ds((group * NX + dx) * per, per)]

    def remote(source, target, ssem, rsem, group, dx, per, forth):
        to = partner(group, dx) if forth else partner(NZ - group, NX - dx)
        return pltpu.make_async_remote_copy(
            src_ref=span(source, group, dx, per),
            dst_ref=span(target, group, dx, per),
            send_sem=ssem.at[group],
            recv_sem=rsem.at[group],
            device_id={"dp": to},
            device_id_type=MESH,
        )

    def keep(source, target, rsem, per):
        return pltpu.make_async_copy(
            span(source, 0, 0, per), span(target, 0, 0, per), rsem.at[0]
        )

    def send(source, target, ssem, rsem, group, per, forth):
        for dx in range(1, NX):
            remote(source, target, ssem, rsem, group, dx, per, forth).start()

        @pl.when(group != 0)
        def _():
            remote(source, target, ssem, rsem, group, 0, per, forth).start()

        @pl.when(group == 0)
        def _():
            keep(source, target, rsem, per).start()

    def arrived(target, rsem, group, per):
        whole = target.at[pl.ds(group * NX * per, NX * per)]
        pltpu.make_async_copy(whole, whole, rsem.at[group]).wait()

    def sent(source, ssem, group, per, blocks):
        whole = source.at[pl.ds(group * NX * per, blocks * per)]
        pltpu.make_async_copy(whole, whole, ssem.at[group]).wait()

    def send_query(group):
        for n in range(PAIR):
            slot = group * PAIR + n
            q_out[slot] = q_perm[idx_s[0, slot]]
        send(q_out, q_got, q_ssem, q_rsem, group, RANKS, True)

    def send_first(step, carry):
        send_query(lax.rem(source_of(step, my_z, -1) - my_z + NZ, NZ))
        return carry

    lax.fori_loop(0, GROUPS, send_first, 0)

    scale = LOG2E / math.sqrt(HD)

    def softmax_values(scores, value_rows):
        highest = jnp.max(scores, axis=1, keepdims=True)
        powers = jnp.exp2(scores - highest)
        total = jnp.sum(powers, axis=1, keepdims=True)
        sums = jnp.dot(powers.astype(jnp.bfloat16), value_rows, preferred_element_type=jnp.float32)
        return sums / total, highest + jnp.log2(total)

    def scores_of(query_rows, key_rows):
        return (
            lax.dot_general(
                query_rows, key_rows, (((1,), (1,)), ((), ())), preferred_element_type=jnp.float32
            )
            * scale
        )

    loads[2].wait()
    loads[3].wait()
    at_row = iota((512, 128), 0)
    at_key = iota((512, 128), 1)
    seen = (at_row // ROWS == at_key // LENGTH) & (at_key % LENGTH <= at_row % LENGTH)

    def own_tokens(n, carry):
        rows = q_perm[pl.ds(n * 16, 16)].reshape(512, HD)
        scores = scores_of(rows, kn[pl.ds(n * 128, 128)])
        scores = jnp.where(seen, scores, MASKED)
        averages, logs = softmax_values(scores, vn[pl.ds(n * 128, 128)])
        own_o[pl.ds(n * 16, 16)] = averages.reshape(16, ROWS, HD)
        own_l[pl.ds(n * 16, 16)] = jnp.broadcast_to(logs, (512, HD)).reshape(16, ROWS, HD)
        return carry

    lax.fori_loop(0, CANDS // 16, own_tokens, 0)

    loads[4].wait()
    loads[5].wait()
    bias[...] = jnp.where(iota((8, PMAX), 1) < plen_ref[0], 0.0, MASKED)
    spread = iota((256, 128), 0) % (RANKS * ROWS) == iota((256, 128), 1)

    def prefix(step, carry):
        group = lax.rem(my_z - source_of(step, my_z, 1) + NZ, NZ)
        arrived(q_got, q_rsem, group, RANKS)
        rows = q_got[pl.ds(group * PAIR, PAIR)].reshape(256, HD)
        scores = scores_of(rows, kc[...]) + bias[0:1, :]
        averages, logs = softmax_values(scores, vc[...])
        m_out[pl.ds(group * PAIR, PAIR)] = averages.astype(jnp.bfloat16).reshape(PAIR, ROWS, HD)
        packed = jnp.where(spread, logs, 0.0).reshape(NX, RANKS * ROWS, HD)
        l_out[pl.ds(group * NX, NX)] = jnp.sum(packed, axis=1, keepdims=True)
        send(m_out, m_got, m_ssem, m_rsem, group, RANKS, False)
        send(l_out, l_got, l_ssem, l_rsem, group, 1, False)
        return carry

    lax.fori_loop(0, GROUPS, prefix, 0)

    def drain_queries(group, carry):
        sent(q_out, q_ssem, group, RANKS, NX)
        return carry

    lax.fori_loop(1, GROUPS, drain_queries, 0)
    sent(q_out, q_ssem, 0, RANKS, NX - 1)

    for load in loads[6:]:
        load.wait()
    weight = gain_ref[...].astype(jnp.float32) * head_ref[...].astype(jnp.float32)
    acc[...] = jnp.zeros_like(acc)
    slot_lane8 = iota((LENGTH, 128), 1)

    def finish(step, carry):
        group = send_order(step)
        arrived(m_got, m_rsem, group, RANKS)
        arrived(l_got, l_rsem, group, 1)
        logs = jnp.broadcast_to(l_got[pl.ds(group * NX, NX)], (NX, RANKS * ROWS, HD))
        logs = jnp.where(spread, logs.reshape(256, HD), 0.0)
        logs = jnp.sum(logs, axis=1, keepdims=True).reshape(PAIR, ROWS, 1)
        squares, dots = acc[0], acc[1]
        for n in range(PAIR):
            slot = group * PAIR + n
            cand = idx_s[0, slot]
            far_log = jnp.broadcast_to(logs[n], (ROWS, HD))
            near_log = own_l[cand]
            top = jnp.maximum(far_log, near_log)
            far, near = jnp.exp2(far_log - top), jnp.exp2(near_log - top)
            mixed = (far * m_got[slot].astype(jnp.float32) + near * own_o[cand]) / (far + near)
            stream = res[cand].astype(jnp.float32)
            square = jnp.zeros((LENGTH, HD), jnp.float32)
            dot = jnp.zeros((LENGTH, HD), jnp.float32)
            for head in range(HEADS):
                hidden = (
                    stream[:, head * HD : (head + 1) * HD]
                    + mixed[head * LENGTH : (head + 1) * LENGTH]
                )
                square += hidden * hidden
                dot += hidden * weight[head : head + 1, :]
            here = slot_lane8 == slot
            squares += jnp.where(here, jnp.sum(square, axis=1, keepdims=True), 0.0)
            dots += jnp.where(here, jnp.sum(dot, axis=1, keepdims=True), 0.0)
        acc[0], acc[1] = squares, dots
        return carry

    lax.fori_loop(0, GROUPS, finish, 0)

    part[my_t] = acc[...]
    shares = []
    for offset in range(1, NT):
        shares.append(
            pltpu.make_async_remote_copy(
                src_ref=acc,
                dst_ref=part.at[my_t],
                send_sem=p_ssem.at[offset],
                recv_sem=p_rsem.at[offset],
                device_id={"tensor": lax.rem(my_t + offset, NT)},
                device_id_type=MESH,
            )
        )
        shares[-1].start()

    def drain(group, carry):
        sent(m_out, m_ssem, group, RANKS, NX)
        sent(l_out, l_ssem, group, 1, NX)
        return carry

    lax.fori_loop(1, GROUPS, drain, 0)
    sent(m_out, m_ssem, 0, RANKS, NX - 1)
    sent(l_out, l_ssem, 0, 1, NX - 1)

    for share in shares:
        share.wait_recv()
    total = part[0]
    for n in range(1, NT):
        total += part[n]
    scored = total[1] * lax.rsqrt(total[0] / FEATURES + EPSILON)
    result = jnp.zeros((LENGTH, CANDS), jnp.float32)
    for _ in range(3):
        piece = scored.astype(jnp.bfloat16)
        scored = scored - piece.astype(jnp.float32)
        result += jnp.dot(piece, place[...], preferred_element_type=jnp.float32)
    inside = iota((LENGTH, CANDS), 0) < len_ref[...]
    out_ref[...] = jnp.where(inside, result, 0.0)

    for share in shares:
        share.wait_send()


def body(
    queries,
    keys_new,
    values_new,
    residual,
    cand_len,
    owner_map,
    prompt_len,
    keys_cache,
    values_cache,
    norm_gain,
    value_head,
):
    bf16, f32 = jnp.bfloat16, jnp.float32
    vmem = pl.BlockSpec(memory_space=pltpu.VMEM)
    hbm = pl.BlockSpec(memory_space=pl.ANY)
    slots = pltpu.VMEM((SLOTS, ROWS, HD), bf16)
    logs = pltpu.VMEM((GROUPS * NX, 1, HD), f32)
    by_group = pltpu.SemaphoreType.DMA((GROUPS,))
    by_offset = pltpu.SemaphoreType.DMA((NT,))
    scored = pl.pallas_call(
        kernel,
        out_shape=jax.ShapeDtypeStruct((LENGTH, CANDS), f32),
        in_specs=[pl.BlockSpec(memory_space=pltpu.SMEM)] + [hbm] * 10,
        out_specs=vmem,
        scratch_shapes=[
            pltpu.VMEM((1, CANDS), jnp.int32),
            pltpu.VMEM((1, CANDS), jnp.int32),
            pltpu.VMEM((HEADS, HD), bf16),
            pltpu.VMEM((HEADS, HD), bf16),
            pltpu.VMEM((CANDS, ROWS, HD), bf16),
            pltpu.VMEM((CANDS * LENGTH, HD), bf16),
            pltpu.VMEM((CANDS * LENGTH, HD), bf16),
            pltpu.VMEM((CANDS, LENGTH, HEADS * HD), bf16),
            pltpu.VMEM((PMAX, HD), bf16),
            pltpu.VMEM((PMAX, HD), bf16),
            pltpu.VMEM((CANDS, ROWS, HD), bf16),
            slots,
            slots,
            slots,
            slots,
            logs,
            logs,
            pltpu.VMEM((CANDS, ROWS, HD), f32),
            pltpu.VMEM((CANDS, ROWS, HD), f32),
            pltpu.VMEM((8, PMAX), f32),
            pltpu.VMEM((8, 128), jnp.int32),
            pltpu.SMEM((8, 128), jnp.int32),
            pltpu.VMEM((SLOTS, CANDS), bf16),
            pltpu.VMEM((2, LENGTH, 128), f32),
            pltpu.VMEM((NT, 2, LENGTH, 128), f32),
            pltpu.SemaphoreType.DMA((10,)),
            pltpu.SemaphoreType.DMA,
            by_group,
            by_group,
            by_group,
            by_group,
            by_group,
            by_group,
            by_offset,
            by_offset,
        ],
        compiler_params=pltpu.CompilerParams(
            collective_id=0, has_side_effects=True, vmem_limit_bytes=62 * 2**20
        ),
    )(
        prompt_len,
        owner_map.reshape(1, CANDS),
        cand_len.reshape(1, CANDS),
        norm_gain.reshape(HEADS, HD),
        value_head.reshape(HEADS, HD),
        queries.reshape(CANDS, ROWS, HD),
        keys_new.reshape(CANDS * LENGTH, HD),
        values_new.reshape(CANDS * LENGTH, HD),
        residual,
        keys_cache.reshape(PMAX, HD),
        values_cache.reshape(PMAX, HD),
    )
    return scored.T


def solution(mesh):
    in_specs = (
        P("dp", None, "tensor", None),
        P("dp", None, "tensor", None),
        P("dp", None, "tensor", None),
        P("dp", None, "tensor"),
        P("dp"),
        P("dp"),
        P("dp"),
        P("dp", None, "tensor", None),
        P("dp", None, "tensor", None),
        P("tensor"),
        P("tensor"),
    )
    out_specs = P("dp", None)
    return jax.shard_map(body, mesh=mesh, in_specs=in_specs, out_specs=out_specs, check_vma=False)
```
